128 devices in a mesh: seq: 32 (over y, x, core), head: 4 (over z).
Axes of the slice: x: 4, y: 4, z: 4, core: 2. Of those that a mesh axis runs over, the one named last changes fastest.
Arguments:
- activations: bfloat16 [32768, 2048], P('seq'), may hold values from -1000 to 1000
- w_qk: bfloat16 [2048, 2048], P(None, 'head'), may hold values from -0.125 to 0.125
- w_value: bfloat16 [2048, 2048], P(None, 'head'), may hold values from -0.125 to 0.125
- w_out: bfloat16 [2048, 2048], P('head'), may hold values from -0.125 to 0.125
- bucket_order: int32 [2, 16, 32768], P(None, 'head', 'seq'), may hold values from 0 to 1023, as said below
- span_sends: int32 [2, 16, 32, 32], P(None, 'head'), may hold values from 0 to 2, as said below
Outputs:
- attended: bfloat16 [32768, 2048], P('seq', 'head')
The draws below stay inside these ranges and needn't reach their ends.
Inputs may be any that keep to these rules, and one draw needn't show every extreme that they name: `bucket_order`: each aligned block of 1024 entries along the last dimension is a permutation of 0 to 1023. span_sends[r, h, s, j] counts the spans of block s that go to bucket range j; for each r, h, s the counts sum to 16. In every round and head one bucket range receives 2 from every block, and every bucket range receives at least one span.
All inputs are finite; a program needn't handle non-finite values.
Results may differ from the reference program's by a relative error of at most 0.015.
The reference program's roundings to bfloat16 on the way count: a program that leaves them out, or rounds other values in their place, can miss the bound.
Values may be sent and summed in bfloat16 or wider, within the bound.
No kernel may reach another device: no remote copies, remote signals or barrier semaphores. Data moves between devices by JAX's collectives and lax.ppermute only.
A program may use at most 192 MiB of HBM per device.

```python
import math
import jax
import jax.numpy as jnp
from jax import lax

D = 2048
HEADS = 16
HEAD_DIM = 128
ROUNDS = 2
SPAN = 64
TOK_DEV = 1024
TOKENS = 32768
SEND_MAX = 2
N_SEQ = 32
N_HEAD = 4


def draw_activations(key, part):
    key = jax.random.fold_in(key, 11)
    return (12.0 * jnp.clip(jax.random.normal(key, (TOKENS, D), jnp.float32), -6.0, 6.0)).astype(jnp.bfloat16)


def draw_bucket_order(key, part):
    key = jax.random.fold_in(key, 23)
    keys = jax.random.split(key, ROUNDS * HEADS * N_SEQ)
    perms = jax.vmap(lambda single: jax.random.permutation(single, TOK_DEV))(keys)
    return perms.reshape(ROUNDS, HEADS, N_SEQ * TOK_DEV).astype(jnp.int32)


def draw_span_sends(key, part):
    key = jax.random.fold_in(key, 37)
    span_count = TOK_DEV // SPAN
    rest = span_count - SEND_MAX
    lowest = max(0, (rest - (N_SEQ - 1) + SEND_MAX - 2) // (SEND_MAX - 1))
    highest = rest // SEND_MAX

    def one_table(single):
        key_busy, key_many, key_rank = jax.random.split(single, 3)
        busy = jax.random.randint(key_busy, (), 0, N_SEQ)
        many = jax.random.randint(key_many, (N_SEQ, 1), lowest, highest + 1)
        ranks = jax.vmap(lambda inner: jax.random.permutation(inner, N_SEQ - 1))(jax.random.split(key_rank, N_SEQ))
        others = jnp.arange(N_SEQ - 1, dtype=jnp.int32)[None, :]
        sources = jnp.arange(N_SEQ, dtype=jnp.int32)[:, None]
        sure = sources % (N_SEQ - 1)
        sure_rank = jnp.take_along_axis(ranks, sure, axis=1)
        ranked = jnp.where(others == sure, 0, jnp.where(ranks < sure_rank, ranks + 1, ranks))
        ones = rest - many * SEND_MAX
        values = jnp.where(ranked < many, SEND_MAX, jnp.where(ranked < many + ones, 1, 0))
        owners = jnp.arange(N_SEQ, dtype=jnp.int32)[None, :]
        other_of = jnp.clip(jnp.where(owners < busy, owners, owners - 1), 0, N_SEQ - 2)
        picked = jnp.take_along_axis(values, jnp.broadcast_to(other_of, (N_SEQ, N_SEQ)), axis=1)
        return jnp.where(owners == busy, SEND_MAX, picked).astype(jnp.int32)
    tables = jax.vmap(one_table)(jax.random.split(key, ROUNDS * HEADS))
    return tables.reshape(ROUNDS, HEADS, N_SEQ, N_SEQ).astype(jnp.int32)


def block_levels(rng, extent, shards, smallest, top_value):
    factor_of = 1.0
    for dim, shards_of in shards:
        draws = jax.random.uniform(jax.random.fold_in(jax.random.fold_in(rng, 6), dim), (shards_of,), jnp.float32, smallest / len(shards), top_value / len(shards))
        factor_of = factor_of * jnp.repeat(jnp.exp(draws), extent[dim] // shards_of).reshape((-1,) + (1,) * (len(extent) - 1 - dim))
    return factor_of


def scatter_about(stream_key, shape, spread, limit, pieces=(), kind=jnp.bfloat16):
    values = spread * jax.random.normal(stream_key, shape, jnp.float32)
    if pieces:
        values = values * block_levels(stream_key, shape, pieces, -0.22, 0.18)
    return jnp.clip(values, -limit, limit).astype(kind)


def setup_inputs(seed: int = 0) -> dict:
    seeds = jax.random.split(jax.random.key(seed), 7)
    return {
        "activations": draw_activations(jax.random.fold_in(seeds[6], 71), 0),
        "w_qk": scatter_about(seeds[1], (D, HEADS * HEAD_DIM), D ** -0.5, 0.125, ((1, 4),)),
        "w_value": scatter_about(seeds[2], (D, HEADS * HEAD_DIM), D ** -0.5, 0.125, ((1, 4),)),
        "w_out": scatter_about(seeds[3], (HEADS * HEAD_DIM, D), (HEADS * HEAD_DIM) ** -0.5, 0.125, ((0, 4),)),
        "bucket_order": draw_bucket_order(jax.random.fold_in(seeds[6], 71), 0),
        "span_sends": draw_span_sends(jax.random.fold_in(seeds[6], 71), 0),
    }


EPS = 1e-06
SELF_SCORE = -100000.0

def stream_tokens(order_row, sends_table):
    span_count = TOK_DEV // SPAN
    bases = (jnp.arange(N_SEQ, dtype=jnp.int32) * TOK_DEV)[:, None]
    tokens = (order_row.reshape(N_SEQ, TOK_DEV) + bases).astype(jnp.int32)
    inclusive = jnp.cumsum(sends_table, axis=1).astype(jnp.int32)
    positions = jnp.arange(span_count, dtype=jnp.int32)
    owners = lax.optimization_barrier(jnp.sum((inclusive[:, None, :] <= positions[None, :, None]).astype(jnp.int32), axis=-1))
    sources = jnp.arange(N_SEQ, dtype=jnp.int32)[:, None]
    sort_key = (owners * (N_SEQ * span_count) + sources * span_count + positions[None, :]).reshape(-1)
    ranking = jnp.argsort(sort_key).astype(jnp.int32)
    return tokens.reshape(N_SEQ * span_count, SPAN)[ranking]

def attend_stream(paired):
    left_rows = jnp.roll(paired, 1, axis=0)
    key_rows = jnp.concatenate([left_rows, paired], axis=1)
    queries = paired[..., :HEAD_DIM].astype(jnp.float32)
    key_part = key_rows[..., :HEAD_DIM].astype(jnp.float32)
    value_part = key_rows[..., HEAD_DIM:].astype(jnp.float32)
    scores = jnp.einsum('cqe,cke->cqk', queries, key_part)
    squares = lax.optimization_barrier(jnp.sum(key_part * key_part, axis=-1))
    scaling = lax.rsqrt(squares + EPS) * (1.0 / math.sqrt(HEAD_DIM))
    scores = scores * scaling[:, None, :]
    query_at = jnp.arange(SPAN, dtype=jnp.int32)[:, None]
    key_at = jnp.arange(2 * SPAN, dtype=jnp.int32)[None, :]
    scores = jnp.where((key_at == query_at + SPAN)[None], jnp.float32(SELF_SCORE), scores)
    summit = lax.optimization_barrier(jnp.max(scores, axis=-1, keepdims=True))
    raised = jnp.exp(scores - summit)
    totals = lax.optimization_barrier(jnp.sum(raised, axis=-1, keepdims=True))
    weights = lax.optimization_barrier((raised / totals).astype(jnp.bfloat16)).astype(jnp.float32)
    mixed = jnp.einsum('cqk,cke->cqe', weights, value_part).astype(jnp.bfloat16)
    log_total = (summit + jnp.log(totals))[..., 0]
    return (mixed, log_total)

def reference(activations, w_qk, w_value, w_out, bucket_order, span_sends):
    keyed = jnp.dot(activations, w_qk, preferred_element_type=jnp.float32).astype(jnp.bfloat16)
    valued = jnp.dot(activations, w_value, preferred_element_type=jnp.float32).astype(jnp.bfloat16)
    columns = []
    for head in range(HEADS):
        lower = head * HEAD_DIM
        paired = jnp.concatenate([keyed[:, lower:lower + HEAD_DIM], valued[:, lower:lower + HEAD_DIM]], axis=1)
        head_outs = []
        head_lses = []
        for round_at in range(ROUNDS):
            chosen = stream_tokens(bucket_order[round_at, head], span_sends[round_at, head])
            mixed, log_total = attend_stream(paired[chosen])
            flattened = chosen.reshape(-1)
            head_outs.append(jnp.zeros((TOKENS, HEAD_DIM), jnp.bfloat16).at[flattened].set(mixed.reshape(-1, HEAD_DIM)))
            head_lses.append(jnp.zeros((TOKENS,), jnp.float32).at[flattened].set(log_total.reshape(-1)))
        stacked = lax.optimization_barrier(jnp.stack(head_outs)).astype(jnp.float32)
        stacked_lse = jnp.stack(head_lses)
        round_peak = lax.optimization_barrier(jnp.max(stacked_lse, axis=0, keepdims=True))
        shares = jnp.exp(stacked_lse - round_peak)
        shares = shares / lax.optimization_barrier(jnp.sum(shares, axis=0, keepdims=True))
        blended = lax.optimization_barrier(jnp.sum(shares[..., None] * stacked, axis=0))
        columns.append(blended.astype(jnp.bfloat16))
    combined = jnp.concatenate(columns, axis=1)
    group_width = HEADS // N_HEAD * HEAD_DIM
    summed = jnp.zeros((TOKENS, D), jnp.float32)
    for group in range(N_HEAD):
        lower = group * group_width
        partial_value = jnp.dot(combined[:, lower:lower + group_width], w_out[lower:lower + group_width], preferred_element_type=jnp.float32).astype(jnp.bfloat16)
        summed = summed + lax.optimization_barrier(partial_value).astype(jnp.float32)
    return summed.astype(jnp.bfloat16)
```

```python
import functools
import math

import jax
import jax.numpy as jnp
from jax import lax
from jax.experimental import pallas as pl
from jax.experimental.pallas import tpu as pltpu
from jax.sharding import PartitionSpec as P

HEAD_DIM = 128
SPAN = 64
EPS = 1e-06
SELF_SCORE = -100000.0
QUARTER = 16
QUARTERS = SPAN // QUARTER
PAIR = 2
SENT = 15
VMEM_LIMIT = 63 * 1024 * 1024


def params(**kwargs):
    return pltpu.CompilerParams(vmem_limit_bytes=VMEM_LIMIT, **kwargs)


def spare_span(sends_ref, r, head, me):
    counts = sends_ref[r, head, pl.ds(me, 1), :].astype(jnp.float32)
    at = lax.broadcasted_iota(jnp.int32, counts.shape, 1).astype(jnp.float32)
    first = jnp.min(jnp.where(counts > 1.5, at, float(counts.shape[1])))
    before = jnp.sum(jnp.where(at < first, counts, 0.0))
    return jnp.clip(before.astype(jnp.int32), 0, SENT - 1)


def sort_kernel(
    me_ref, sends_ref, act_ref, wq_ref, wv_ref, order_ref, out_ref, sent_ref, kv_ref, onehot_ref
):
    tokens = act_ref.shape[0]
    spans = tokens // SPAN
    rounds = out_ref.shape[0]
    head = pl.program_id(0)
    lanes = 128
    token_at = lax.broadcasted_iota(jnp.int32, (lanes, tokens), 1).astype(jnp.float32)
    for r in range(rounds):
        row = order_ref[r, pl.ds(head, 1), :].astype(jnp.float32)
        parts = [row[:, j : j + lanes] for j in range(0, tokens, lanes)]
        wanted = jnp.concatenate(parts, axis=0).T
        for j in range(tokens // lanes):
            onehot = jnp.where(wanted[:, j : j + 1] == token_at, 1.0, 0.0)
            onehot_ref[r, j * lanes : (j + 1) * lanes, :] = onehot.astype(jnp.bfloat16)
    weights = jnp.concatenate([wq_ref[...], wv_ref[...]], axis=1)
    kv_ref[...] = jnp.dot(
        act_ref[...], weights, preferred_element_type=jnp.float32
    ).astype(jnp.bfloat16)

    def one_round(r, carry):
        rows = jnp.dot(onehot_ref[r], kv_ref[...], preferred_element_type=jnp.float32)
        rows = rows.astype(jnp.bfloat16)
        for at in range(2):
            half = rows[:, at * HEAD_DIM : (at + 1) * HEAD_DIM]
            half = half.reshape(spans, QUARTERS, QUARTER, HEAD_DIM)
            for quarter in range(QUARTERS):
                out_ref[r, 0, at, quarter, 0] = half[:, quarter]
        spare = spare_span(sends_ref, r, head, me_ref[0])
        for at in range(2):
            tiles = [
                out_ref[r, 0, at, :, 0, j + (j >= spare).astype(jnp.int32)] for j in range(SENT)
            ]
            for j, tile in enumerate(tiles):
                sent_ref[r, 0, at, :, 0, j] = tile
        return carry

    lax.fori_loop(0, rounds, one_round, 0)


def project_and_sort(me, sends, activations, w_qk, w_value, order):
    tokens, width = activations.shape
    rounds, heads = order.shape[:2]
    block = (rounds, 1, 2, QUARTERS, 1, tokens // SPAN, QUARTER, HEAD_DIM)
    shape = (rounds, PAIR, 2, QUARTERS, heads // PAIR) + block[5:]
    return pl.pallas_call(
        sort_kernel,
        grid=(heads,),
        in_specs=[
            pl.BlockSpec(memory_space=pltpu.SMEM),
            pl.BlockSpec(sends.shape, lambda h: (0, 0, 0, 0)),
            pl.BlockSpec((tokens, width), lambda h: (0, 0)),
            pl.BlockSpec((width, HEAD_DIM), lambda h: (0, h)),
            pl.BlockSpec((width, HEAD_DIM), lambda h: (0, h)),
            pl.BlockSpec(order.shape, lambda h: (0, 0, 0)),
        ],
        out_specs=[
            pl.BlockSpec(block, lambda h: (0, h % PAIR, 0, 0, h // PAIR, 0, 0, 0)),
            pl.BlockSpec(
                block[:5] + (SENT,) + block[6:],
                lambda h: (0, h % PAIR, 0, 0, h // PAIR, 0, 0, 0),
            ),
        ],
        out_shape=[
            jax.ShapeDtypeStruct(shape, jnp.bfloat16),
            jax.ShapeDtypeStruct(shape[:5] + (SENT,) + shape[6:], jnp.bfloat16),
        ],
        scratch_shapes=[
            pltpu.VMEM((tokens, 2 * HEAD_DIM), jnp.bfloat16),
            pltpu.VMEM((rounds, tokens, tokens), jnp.bfloat16),
        ],
        compiler_params=params(),
        cost_estimate=pl.CostEstimate(
            flops=heads * tokens * 4 * HEAD_DIM * (width + rounds * tokens),
            bytes_accessed=2 * tokens * width + heads * 4 * HEAD_DIM * (width + 2 * tokens),
            transcendentals=0,
        ),
    )(me, sends, activations, w_qk, w_value, order)


def left_table(counts):
    blocks, ranges = counts.shape[1:]
    spans = SENT + 1
    at = jnp.arange(ranges, dtype=jnp.int32)
    block_at = jnp.arange(blocks, dtype=jnp.int32)
    upto = at[:, None] <= at[None, :]
    inclusive = jnp.sum(jnp.where(upto[None, None], counts[:, :, :, None], 0), axis=2)
    exclusive = inclusive - counts
    spare = jnp.min(jnp.where(counts > 1, exclusive, SENT - 1), axis=2)[:, :, None]
    ends = inclusive - 1
    ends = block_at[None, :, None] * spans + ends - (ends > spare).astype(jnp.int32)
    tails = jnp.where(counts > 0, ends, -1)
    earlier = block_at[:, None] < block_at[None, :]
    before = jnp.max(
        jnp.where(earlier[None, :, :, None], tails[:, :, None, :], -1), axis=1
    )
    last = jnp.max(tails, axis=1)
    wrapped = jnp.roll(last, 1, axis=-1)
    before = jnp.where(before < 0, wrapped[:, None, :], before)
    k_at = jnp.arange(SENT, dtype=jnp.int32)[None, None, :]
    k_at = k_at + (k_at > spare).astype(jnp.int32)
    here = k_at - 1
    here = block_at[None, :, None] * spans + here - (here > spare).astype(jnp.int32)
    k_at, here = k_at[..., None], here[..., None]
    first = exclusive[:, :, None, :]
    mine = (first <= k_at) & (k_at < inclusive[:, :, None, :])
    left = jnp.where(k_at > first, here, before[:, :, None, :])
    left = jnp.sum(jnp.where(mine, left, 0), axis=-1)
    return jnp.clip(left, 0, blocks * spans - 2).reshape(counts.shape[0], blocks * SENT)


def permute_kernel(pair, table_ref, in_ref, out_ref):
    steps, sent = out_ref.shape[:2]
    start = pl.program_id(0) * steps

    def one_block(t, carry):
        tiles = []
        for k in range(sent):
            place = table_ref[pair, (start + t) * sent + k]
            tiles.append(in_ref[place >> 4, 0, place & 15])
        for k, tile in enumerate(tiles):
            out_ref[t, k] = tile
        return carry

    lax.fori_loop(0, steps, one_block, 0)


def permute(table, pieces, pair):
    blocks, _, sent, rows, columns = pieces.shape
    steps = 4
    size = blocks * sent * rows * columns
    return pl.pallas_call(
        functools.partial(permute_kernel, pair),
        grid=(steps,),
        in_specs=[
            pl.BlockSpec(memory_space=pltpu.SMEM),
            pl.BlockSpec((blocks, 1, sent, rows, columns), lambda i: (0, pair, 0, 0, 0)),
        ],
        out_specs=pl.BlockSpec((blocks // steps, sent, rows, columns), lambda i: (i, 0, 0, 0)),
        out_shape=jax.ShapeDtypeStruct((blocks, sent, rows, columns), jnp.bfloat16),
        compiler_params=params(),
        cost_estimate=pl.CostEstimate(flops=size, bytes_accessed=4 * size, transcendentals=0),
    )(table, pieces)


def as_spans(quarters):
    spans = quarters.shape[1]
    return jnp.swapaxes(quarters, 0, 1).reshape(spans, SPAN, HEAD_DIM)


def batched(left, right, left_dim, right_dim):
    return lax.dot_general(
        left,
        right,
        (((left_dim,), (right_dim,)), ((0,), (0,))),
        preferred_element_type=jnp.float32,
    )


def attend_kernel(
    first, me_ref, sends_ref, own_ref, left_ref, order_ref, lower_ref, upper_ref, mixed_ref, all_ref
):
    rounds, _, tokens = order_ref.shape
    head = first + pl.program_id(0)
    spans = tokens // SPAN
    for r in range(rounds):
        spare = spare_span(sends_ref, r, head, me_ref[0])
        for at in range(2):
            tiles = [left_ref[r, 0, at, :, j] for j in range(SENT)]
            tiles.append(own_ref[r, 0, at, :, 0, spare])
            for j, tile in enumerate(tiles[:-1]):
                all_ref[r, at, :, j + (j > spare).astype(jnp.int32)] = tile
            all_ref[r, at, :, spare + 1] = tiles[-1]
        queries = as_spans(own_ref[r, 0, 0, :, 0])
        keys = jnp.concatenate([as_spans(all_ref[r, 0]), queries], axis=1)
        values = jnp.concatenate([as_spans(all_ref[r, 1]), as_spans(own_ref[r, 0, 1, :, 0])], axis=1)
        scores = batched(queries, keys, 2, 2)
        wide = keys.astype(jnp.float32)
        squares = wide * wide
        high = squares.astype(jnp.bfloat16)
        low = (squares - high.astype(jnp.float32)).astype(jnp.bfloat16)
        ones = jnp.ones((spans, 16, 2 * HEAD_DIM), jnp.bfloat16)
        sums = batched(ones, jnp.concatenate([high, low], axis=2), 2, 2)
        scaling = lax.rsqrt(sums[:, :1, :] + EPS) * (1.0 / math.sqrt(HEAD_DIM))
        scores = scores * scaling
        query_at = lax.broadcasted_iota(jnp.int32, scores.shape, 1)
        key_at = lax.broadcasted_iota(jnp.int32, scores.shape, 2)
        scores = jnp.where(key_at == query_at + SPAN, SELF_SCORE, scores)
        summit = jnp.max(scores, axis=-1, keepdims=True)
        raised = jnp.exp(scores - summit)
        totals = jnp.sum(raised, axis=-1, keepdims=True)
        weights = (raised * (1.0 / totals)).astype(jnp.bfloat16)
        mixed = batched(weights, values, 2, 1).astype(jnp.bfloat16)
        log_total = summit + jnp.log(totals)
        high = log_total.astype(jnp.bfloat16).astype(jnp.float32)
        middle = (log_total - high).astype(jnp.bfloat16).astype(jnp.float32)
        low = log_total - high - middle
        lane = lax.broadcasted_iota(jnp.int32, scores.shape, 2)
        terms = jnp.where(lane == 0, high, jnp.where(lane == 1, middle, low))
        terms = jnp.where(lane < 3, terms, 0.0).astype(jnp.bfloat16)
        mixed_ref[r, :, :HEAD_DIM] = mixed.reshape(tokens, HEAD_DIM)
        mixed_ref[r, :, HEAD_DIM:] = terms.reshape(tokens, HEAD_DIM)
    step = 256
    token_at = lax.broadcasted_iota(jnp.int32, (step, tokens), 0)
    for lower in range(0, tokens, step):
        rows, totals = [], []
        for r in range(rounds):
            onehot = order_ref[r, pl.ds(head, 1), :] == token_at + lower
            onehot = jnp.where(onehot, 1.0, 0.0).astype(jnp.bfloat16)
            found = jnp.dot(onehot, mixed_ref[r], preferred_element_type=jnp.float32)
            rows.append(found[:, :HEAD_DIM])
            totals.append(
                found[:, HEAD_DIM : HEAD_DIM + 1]
                + found[:, HEAD_DIM + 1 : HEAD_DIM + 2]
                + found[:, HEAD_DIM + 2 : HEAD_DIM + 3]
            )
        peak = functools.reduce(jnp.maximum, totals)
        shares = [jnp.exp(total - peak) for total in totals]
        inverse = 1.0 / functools.reduce(jnp.add, shares)
        blended = functools.reduce(
            jnp.add, [(share * inverse) * row for share, row in zip(shares, rows)]
        )
        out_ref = lower_ref if lower < tokens // 2 else upper_ref
        at = lower % (tokens // 2)
        out_ref[at : at + step, :] = blended.astype(jnp.bfloat16)


def attend(me, sends, own, left, order, pair):
    rounds, _, tokens = order.shape
    block = (rounds, 1, 2, QUARTERS, 1) + own.shape[5:]
    half = jax.ShapeDtypeStruct((tokens // 2, PAIR * HEAD_DIM), jnp.bfloat16)
    return pl.pallas_call(
        functools.partial(attend_kernel, PAIR * pair),
        grid=(PAIR,),
        in_specs=[
            pl.BlockSpec(memory_space=pltpu.SMEM),
            pl.BlockSpec(sends.shape, lambda h: (0, 0, 0, 0)),
            pl.BlockSpec(block, lambda h: (0, h, 0, 0, pair, 0, 0, 0)),
            pl.BlockSpec(block[:4] + left.shape[1:], lambda h: (0, h, 0, 0, 0, 0, 0)),
            pl.BlockSpec(order.shape, lambda h: (0, 0, 0)),
        ],
        out_specs=[pl.BlockSpec((tokens // 2, HEAD_DIM), lambda h: (0, h))] * 2,
        out_shape=[half, half],
        scratch_shapes=[
            pltpu.VMEM((rounds, tokens, 2 * HEAD_DIM), jnp.bfloat16),
            pltpu.VMEM((rounds, 2, QUARTERS) + own.shape[5:], jnp.bfloat16),
        ],
        compiler_params=params(),
        cost_estimate=pl.CostEstimate(
            flops=PAIR * rounds * tokens * 4 * HEAD_DIM * (tokens + 2 * SPAN),
            bytes_accessed=PAIR * rounds * tokens * 8 * HEAD_DIM,
            transcendentals=PAIR * rounds * tokens * 2 * SPAN,
        ),
    )(me, sends, own, left.reshape(own.shape[:4] + left.shape[1:]), order)


def output_kernel(started, *refs):
    out_ref = refs[-1]
    lower_half = pl.program_id(0) < pl.num_programs(0) // 2
    total = refs[0][...] if started else jnp.zeros(out_ref.shape, jnp.float32)
    for at in range(int(started), len(refs) - 1, 3):
        w_ref, lower_ref, upper_ref = refs[at : at + 3]
        rows = jnp.where(lower_half, lower_ref[...], upper_ref[...])
        total += jnp.dot(rows, w_ref[0], preferred_element_type=jnp.float32)
    out_ref[...] = total.astype(out_ref.dtype)


def project_out(weights, started, terms):
    columns = weights.shape[2]
    half, depth = terms[0][2].shape
    tokens = 2 * half
    steps = 4
    step = tokens // steps
    lower = lambda i: (jnp.minimum(i, steps // 2 - 1), 0)
    upper = lambda i: (jnp.maximum(i - steps // 2, 0), 0)
    in_specs, operands = [], []
    if started is not None:
        in_specs.append(pl.BlockSpec((step, columns), lambda i: (i, 0)))
        operands.append(started)
    for pair, behind, lower_rows, upper_rows in terms:
        in_specs += [
            pl.BlockSpec((1, depth, columns), lambda i, at=(behind, pair, 0): at),
            pl.BlockSpec((step, depth), lower),
            pl.BlockSpec((step, depth), upper),
        ]
        operands += [weights, lower_rows, upper_rows]
    kind = jnp.float32 if started is None else jnp.bfloat16
    return pl.pallas_call(
        functools.partial(output_kernel, started is not None),
        grid=(steps,),
        in_specs=in_specs,
        out_specs=pl.BlockSpec((step, columns), lambda i: (i, 0)),
        out_shape=jax.ShapeDtypeStruct((tokens, columns), kind),
        compiler_params=params(),
        cost_estimate=pl.CostEstimate(
            flops=2 * len(terms) * tokens * depth * columns,
            bytes_accessed=2 * len(terms) * depth * (tokens + columns) + 6 * tokens * columns,
            transcendentals=0,
        ),
    )(*operands)


def passed(array, by):
    count = lax.axis_size("head")
    return lax.ppermute(array, "head", [(i, (i + by) % count) for i in range(count)])


def from_all_groups(lower, upper, meanwhile=None):
    lower_behind = passed(lower, 1)
    upper_ahead = passed(upper, -1)
    upper_behind = passed(upper, 1)
    lower_ahead = passed(lower, -1)
    if meanwhile is not None:
        lower_behind, upper_ahead, meanwhile = lax.optimization_barrier(
            (lower_behind, upper_ahead, meanwhile)
        )
    lower_opposite = passed(lower_behind, 1)
    upper_opposite = passed(upper_ahead, -1)
    return meanwhile, [
        (0, lower, upper),
        (1, lower_behind, upper_behind),
        (3, lower_ahead, upper_ahead),
        (2, lower_opposite, upper_opposite),
    ]


def after(array, terms):
    array, rows = lax.optimization_barrier((array, [term[2:] for term in terms]))
    return array, [term[:2] + row for term, row in zip(terms, rows)]


def body(activations, w_qk, w_value, w_out, bucket_order, span_sends):
    seq_count = lax.axis_size("seq")
    head_count = lax.axis_size("head")
    my_seq = lax.axis_index("seq")
    my_head = lax.axis_index("head")
    me = my_seq.reshape(1).astype(jnp.int32)
    pairs = bucket_order.shape[1] // PAIR
    columns = w_out.shape[1] // head_count

    def send(pieces):
        return lax.all_to_all(pieces, "seq", split_axis=0, concat_axis=0, tiled=True)

    own, sent = project_and_sort(me, span_sends, activations, w_qk, w_value, bucket_order)
    arrived = send(sent.reshape(seq_count, pairs, SENT, QUARTER, HEAD_DIM))

    blocks = []
    for shift in range(head_count):
        at = lax.rem(my_head + shift, head_count) * columns
        block = lax.dynamic_slice_in_dim(w_out, at, columns, axis=1)
        blocks.append(passed(block, shift) if shift else block)
    weights = jnp.stack(blocks)

    of_round = span_sends[my_seq // (2 * PAIR * QUARTERS)]
    of_round = of_round.reshape((pairs, PAIR) + of_round.shape[1:])
    table = left_table(of_round[:, my_seq // (2 * QUARTERS) % PAIR])
    left = []
    for pair in range(pairs):
        pieces = permute(table, arrived, pair)
        pieces, arrived, weights = lax.optimization_barrier((pieces, arrived, weights))
        left.append(send(pieces))

    started, terms = None, []
    for pair in range(pairs):
        if terms:
            left[pair], terms = after(left[pair], terms)
        halves = attend(me, span_sends, own, left[pair], bucket_order, pair)
        if terms:
            started = project_out(weights, None, terms + [(pair, 0, *halves)])
        started, gathered = from_all_groups(*halves, started)
        terms = [(pair,) + term for term in gathered]
    return project_out(weights, started, terms[1:])


def solution(mesh):
    in_specs = (
        P("seq", None),
        P(None, "head"),
        P(None, "head"),
        P("head", None),
        P(None, "head", "seq"),
        P(None, "head", None, None),
    )
    out_specs = P("seq", "head")
    return jax.shard_map(body, mesh=mesh, in_specs=in_specs, out_specs=out_specs, check_vma=False)
```

```python
import functools
import math

import jax
import jax.numpy as jnp
from jax import lax
from jax.experimental import pallas as pl
from jax.experimental.pallas import tpu as pltpu
from jax.sharding import PartitionSpec as P

HEAD_DIM = 128
SPAN = 64
EPS = 1e-06
SELF_SCORE = -100000.0
QUARTER = 16
QUARTERS = SPAN // QUARTER
PAIR = 2
SENT = 15
VMEM_LIMIT = 64 * 1024 * 1024
OUTPUT_LIMIT = 24 * 1024 * 1024


def params(limit=VMEM_LIMIT):
    return pltpu.CompilerParams(vmem_limit_bytes=limit)


def spare_span(sends_ref, r, head, me):
    counts = sends_ref[r, head, pl.ds(me, 1), :].astype(jnp.float32)
    at = lax.broadcasted_iota(jnp.int32, counts.shape, 1).astype(jnp.float32)
    first = jnp.min(jnp.where(counts > 1.5, at, float(counts.shape[1])))
    before = jnp.sum(jnp.where(at < first, counts, 0.0))
    return jnp.clip(before.astype(jnp.int32), 0, SENT - 1)


def sort_kernel(
    first, me_ref, sends_ref, act_ref, wq_ref, wv_ref, order_ref, out_ref, sent_ref, kv_ref, onehot_ref
):
    tokens = act_ref.shape[0]
    spans = tokens // SPAN
    rounds = out_ref.shape[0]
    head = first + pl.program_id(0)
    lanes = 128
    token_at = lax.broadcasted_iota(jnp.int32, (lanes, tokens), 1).astype(jnp.float32)
    for r in range(rounds):
        row = order_ref[r, pl.ds(head, 1), :].astype(jnp.float32)
        parts = [row[:, j : j + lanes] for j in range(0, tokens, lanes)]
        wanted = jnp.concatenate(parts, axis=0).T
        for j in range(tokens // lanes):
            onehot = jnp.where(wanted[:, j : j + 1] == token_at, 1.0, 0.0)
            onehot_ref[r, j * lanes : (j + 1) * lanes, :] = onehot.astype(jnp.bfloat16)
    weights = jnp.concatenate([wq_ref[...], wv_ref[...]], axis=1)
    kv_ref[...] = jnp.dot(
        act_ref[...], weights, preferred_element_type=jnp.float32
    ).astype(jnp.bfloat16)

    def one_round(r, carry):
        rows = jnp.dot(onehot_ref[r], kv_ref[...], preferred_element_type=jnp.float32)
        rows = rows.astype(jnp.bfloat16)
        for at in range(2):
            half = rows[:, at * HEAD_DIM : (at + 1) * HEAD_DIM]
            half = half.reshape(spans, QUARTERS, QUARTER, HEAD_DIM)
            for quarter in range(QUARTERS):
                out_ref[r, 0, at, quarter, 0] = half[:, quarter]
        spare = spare_span(sends_ref, r, head, me_ref[0])
        for at in range(2):
            tiles = [
                out_ref[r, 0, at, :, 0, j + (j >= spare).astype(jnp.int32)] for j in range(SENT)
            ]
            for j, tile in enumerate(tiles):
                sent_ref[r, 0, at, :, 0, j] = tile
        return carry

    lax.fori_loop(0, rounds, one_round, 0)


def project_and_sort(me, sends, activations, w_qk, w_value, order, pair):
    tokens, width = activations.shape
    rounds, heads = order.shape[0], PAIR
    first = PAIR * pair
    block = (rounds, 1, 2, QUARTERS, 1, tokens // SPAN, QUARTER, HEAD_DIM)
    shape = (rounds, PAIR, 2, QUARTERS, heads // PAIR) + block[5:]
    return pl.pallas_call(
        functools.partial(sort_kernel, first),
        grid=(heads,),
        in_specs=[
            pl.BlockSpec(memory_space=pltpu.SMEM),
            pl.BlockSpec(sends.shape, lambda h: (0, 0, 0, 0)),
            pl.BlockSpec((tokens, width), lambda h: (0, 0)),
            pl.BlockSpec((width, HEAD_DIM), lambda h: (0, first + h)),
            pl.BlockSpec((width, HEAD_DIM), lambda h: (0, first + h)),
            pl.BlockSpec(order.shape, lambda h: (0, 0, 0)),
        ],
        out_specs=[
            pl.BlockSpec(block, lambda h: (0, h % PAIR, 0, 0, h // PAIR, 0, 0, 0)),
            pl.BlockSpec(
                block[:5] + (SENT,) + block[6:],
                lambda h: (0, h % PAIR, 0, 0, h // PAIR, 0, 0, 0),
            ),
        ],
        out_shape=[
            jax.ShapeDtypeStruct(shape, jnp.bfloat16),
            jax.ShapeDtypeStruct(shape[:5] + (SENT,) + shape[6:], jnp.bfloat16),
        ],
        scratch_shapes=[
            pltpu.VMEM((tokens, 2 * HEAD_DIM), jnp.bfloat16),
            pltpu.VMEM((rounds, tokens, tokens), jnp.bfloat16),
        ],
        compiler_params=params(),
        cost_estimate=pl.CostEstimate(
            flops=heads * tokens * 4 * HEAD_DIM * (width + rounds * tokens),
            bytes_accessed=2 * tokens * width + heads * 4 * HEAD_DIM * (width + 2 * tokens),
            transcendentals=0,
        ),
    )(me, sends, activations, w_qk, w_value, order)


def left_table(counts):
    blocks, ranges = counts.shape[1:]
    spans = SENT + 1
    at = jnp.arange(ranges, dtype=jnp.int32)
    block_at = jnp.arange(blocks, dtype=jnp.int32)
    upto = at[:, None] <= at[None, :]
    inclusive = jnp.sum(jnp.where(upto[None, None], counts[:, :, :, None], 0), axis=2)
    exclusive = inclusive - counts
    spare = jnp.min(jnp.where(counts > 1, exclusive, SENT - 1), axis=2)[:, :, None]
    ends = inclusive - 1
    ends = block_at[None, :, None] * spans + ends - (ends > spare).astype(jnp.int32)
    tails = jnp.where(counts > 0, ends, -1)
    earlier = block_at[:, None] < block_at[None, :]
    before = jnp.max(
        jnp.where(earlier[None, :, :, None], tails[:, :, None, :], -1), axis=1
    )
    last = jnp.max(tails, axis=1)
    wrapped = jnp.roll(last, 1, axis=-1)
    before = jnp.where(before < 0, wrapped[:, None, :], before)
    k_at = jnp.arange(SENT, dtype=jnp.int32)[None, None, :]
    k_at = k_at + (k_at > spare).astype(jnp.int32)
    here = k_at - 1
    here = block_at[None, :, None] * spans + here - (here > spare).astype(jnp.int32)
    k_at, here = k_at[..., None], here[..., None]
    first = exclusive[:, :, None, :]
    mine = (first <= k_at) & (k_at < inclusive[:, :, None, :])
    left = jnp.where(k_at > first, here, before[:, :, None, :])
    left = jnp.sum(jnp.where(mine, left, 0), axis=-1)
    return jnp.clip(left, 0, blocks * spans - 2).reshape(counts.shape[0], blocks * SENT)


def permute_kernel(pair, table_ref, in_ref, out_ref):
    steps, sent = out_ref.shape[:2]
    start = pl.program_id(0) * steps

    def one_block(t, carry):
        tiles = []
        for k in range(sent):
            place = table_ref[pair, (start + t) * sent + k]
            tiles.append(in_ref[place >> 4, 0, place & 15])
        for k, tile in enumerate(tiles):
            out_ref[t, k] = tile
        return carry

    lax.fori_loop(0, steps, one_block, 0, unroll=4)


def permute(table, pieces, pair):
    blocks, _, sent, rows, columns = pieces.shape
    steps = 2
    size = blocks * sent * rows * columns
    return pl.pallas_call(
        functools.partial(permute_kernel, pair),
        grid=(steps,),
        in_specs=[
            pl.BlockSpec(memory_space=pltpu.SMEM),
            pl.BlockSpec((blocks, 1, sent, rows, columns), lambda i: (0, 0, 0, 0, 0)),
        ],
        out_specs=pl.BlockSpec((blocks // steps, sent, rows, columns), lambda i: (i, 0, 0, 0)),
        out_shape=jax.ShapeDtypeStruct((blocks, sent, rows, columns), jnp.bfloat16),
        compiler_params=params(),
        cost_estimate=pl.CostEstimate(flops=size, bytes_accessed=4 * size, transcendentals=0),
    )(table, pieces)


def as_spans(quarters):
    spans = quarters.shape[1]
    return jnp.swapaxes(quarters, 0, 1).reshape(spans, SPAN, HEAD_DIM)


def batched(left, right, left_dim, right_dim):
    return lax.dot_general(
        left,
        right,
        (((left_dim,), (right_dim,)), ((0,), (0,))),
        preferred_element_type=jnp.float32,
    )


def attend_kernel(
    first, me_ref, sends_ref, own_ref, left_ref, order_ref, *refs
):
    *out_refs, mixed_ref, all_ref = refs
    rounds, _, tokens = order_ref.shape
    head = first + pl.program_id(0)
    spans = tokens // SPAN
    for r in range(rounds):
        spare = spare_span(sends_ref, r, head, me_ref[0])
        for at in range(2):
            tiles = [left_ref[r, 0, at, :, j] for j in range(SENT)]
            tiles.append(own_ref[r, 0, at, :, 0, spare])
            for j, tile in enumerate(tiles[:-1]):
                all_ref[r, at, :, j + (j > spare).astype(jnp.int32)] = tile
            all_ref[r, at, :, spare + 1] = tiles[-1]
        queries = as_spans(own_ref[r, 0, 0, :, 0])
        keys = jnp.concatenate([as_spans(all_ref[r, 0]), queries], axis=1)
        values = jnp.concatenate([as_spans(all_ref[r, 1]), as_spans(own_ref[r, 0, 1, :, 0])], axis=1)
        scores = batched(queries, keys, 2, 2)
        wide = keys.astype(jnp.float32)
        squares = wide * wide
        sums = jnp.sum(squares, axis=2)[:, None, :]
        scaling = lax.rsqrt(sums + EPS) * (1.0 / math.sqrt(HEAD_DIM))
        scores = scores * scaling
        query_at = lax.broadcasted_iota(jnp.int32, scores.shape, 1)
        key_at = lax.broadcasted_iota(jnp.int32, scores.shape, 2)
        scores = jnp.where(key_at == query_at + SPAN, SELF_SCORE, scores)
        summit = jnp.max(scores, axis=-1, keepdims=True)
        raised = jnp.exp(scores - summit)
        totals = jnp.sum(raised, axis=-1, keepdims=True)
        weights = (raised * (1.0 / totals)).astype(jnp.bfloat16)
        mixed = batched(weights, values, 2, 1).astype(jnp.bfloat16)
        log_total = summit + jnp.log(totals)
        high = log_total.astype(jnp.bfloat16).astype(jnp.float32)
        middle = (log_total - high).astype(jnp.bfloat16).astype(jnp.float32)
        low = log_total - high - middle
        lane = lax.broadcasted_iota(jnp.int32, scores.shape, 2)
        terms = jnp.where(lane == 0, high, jnp.where(lane == 1, middle, low))
        terms = jnp.where(lane < 3, terms, 0.0).astype(jnp.bfloat16)
        mixed_ref[r, :, :HEAD_DIM] = mixed.reshape(tokens, HEAD_DIM)
        mixed_ref[r, :, HEAD_DIM:] = terms.reshape(tokens, HEAD_DIM)
    step = 256
    token_at = lax.broadcasted_iota(jnp.int32, (step, tokens), 0)
    for lower in range(0, tokens, step):
        rows, totals = [], []
        for r in range(rounds):
            onehot = order_ref[r, pl.ds(head, 1), :] == token_at + lower
            onehot = jnp.where(onehot, 1.0, 0.0).astype(jnp.bfloat16)
            found = jnp.dot(onehot, mixed_ref[r], preferred_element_type=jnp.float32)
            rows.append(found[:, :HEAD_DIM])
            totals.append(
                found[:, HEAD_DIM : HEAD_DIM + 1]
                + found[:, HEAD_DIM + 1 : HEAD_DIM + 2]
                + found[:, HEAD_DIM + 2 : HEAD_DIM + 3]
            )
        peak = functools.reduce(jnp.maximum, totals)
        shares = [jnp.exp(total - peak) for total in totals]
        inverse = 1.0 / functools.reduce(jnp.add, shares)
        blended = functools.reduce(
            jnp.add, [(share * inverse) * row for share, row in zip(shares, rows)]
        )
        share = tokens // len(out_refs)
        out_ref, at = out_refs[lower // share], lower % share
        out_ref[at : at + step, :] = blended.astype(jnp.bfloat16)


def attend(me, sends, own, left, order, pair, parts):
    rounds, _, tokens = order.shape
    block = (rounds, 1, 2, QUARTERS, 1) + own.shape[5:]
    share = tokens // parts
    part = jax.ShapeDtypeStruct((share, PAIR * HEAD_DIM), jnp.bfloat16)
    return pl.pallas_call(
        functools.partial(attend_kernel, PAIR * pair),
        grid=(PAIR,),
        in_specs=[
            pl.BlockSpec(memory_space=pltpu.SMEM),
            pl.BlockSpec(sends.shape, lambda h: (0, 0, 0, 0)),
            pl.BlockSpec(block, lambda h: (0, h, 0, 0, 0, 0, 0, 0)),
            pl.BlockSpec(block[:4] + left.shape[1:], lambda h: (0, h, 0, 0, 0, 0, 0)),
            pl.BlockSpec(order.shape, lambda h: (0, 0, 0)),
        ],
        out_specs=[pl.BlockSpec((share, HEAD_DIM), lambda h: (0, h))] * parts,
        out_shape=[part] * parts,
        scratch_shapes=[
            pltpu.VMEM((rounds, tokens, 2 * HEAD_DIM), jnp.bfloat16),
            pltpu.VMEM((rounds, 2, QUARTERS) + own.shape[5:], jnp.bfloat16),
        ],
        compiler_params=params(),
        cost_estimate=pl.CostEstimate(
            flops=PAIR * rounds * tokens * 4 * HEAD_DIM * (tokens + 2 * SPAN),
            bytes_accessed=PAIR * rounds * tokens * 8 * HEAD_DIM,
            transcendentals=PAIR * rounds * tokens * 2 * SPAN,
        ),
    )(me, sends, own, left.reshape(own.shape[:4] + left.shape[1:]), order)


def output_kernel(started, parts, *refs):
    out_ref = refs[-1]
    lower_half = pl.program_id(0) < pl.num_programs(0) // 2
    total = refs[0][...] if started else jnp.zeros(out_ref.shape, jnp.float32)
    at = int(started)
    for count in parts:
        rows = refs[at + 1][...]
        if count == 2:
            rows = jnp.where(lower_half, rows, refs[at + 2][...])
        total += jnp.dot(rows, refs[at][0], preferred_element_type=jnp.float32)
        at += 1 + count
    out_ref[...] = total.astype(out_ref.dtype)


def project_out(weights, started, terms):
    columns = weights.shape[2]
    tokens = sum(rows.shape[0] for rows in terms[0][2])
    depth = terms[0][2][0].shape[1]
    steps = 2
    step = tokens // steps
    whole = lambda i: (i, 0)
    lower = lambda i: (jnp.minimum(i, steps // 2 - 1), 0)
    upper = lambda i: (jnp.maximum(i - steps // 2, 0), 0)
    in_specs, operands = [], []
    if started is not None:
        in_specs.append(pl.BlockSpec((step, columns), whole))
        operands.append(started)
    for pair, behind, rows in terms:
        in_specs.append(pl.BlockSpec((1, depth, columns), lambda i, at=(behind, pair, 0): at))
        for where in [whole] if len(rows) == 1 else [lower, upper]:
            in_specs.append(pl.BlockSpec((step, depth), where))
        operands += [weights, *rows]
    kind = jnp.float32 if started is None else jnp.bfloat16
    return pl.pallas_call(
        functools.partial(output_kernel, started is not None, [len(t[2]) for t in terms]),
        grid=(steps,),
        in_specs=in_specs,
        out_specs=pl.BlockSpec((step, columns), whole),
        out_shape=jax.ShapeDtypeStruct((tokens, columns), kind),
        compiler_params=params(OUTPUT_LIMIT),
        cost_estimate=pl.CostEstimate(
            flops=2 * len(terms) * tokens * depth * columns,
            bytes_accessed=2 * len(terms) * depth * (tokens + columns) + 6 * tokens * columns,
            transcendentals=0,
        ),
    )(*operands)


def passed(array, by):
    count = lax.axis_size("head")
    return lax.ppermute(array, "head", [(i, (i + by) % count) for i in range(count)])


def from_all_groups(mine):
    return [(0, [mine]), (1, [passed(mine, 1)]), (3, [passed(mine, -1)]), (2, [passed(mine, 2)])]


def round_the_ring(lower, upper, meanwhile):
    lower_behind = passed(lower, 1)
    upper_ahead = passed(upper, -1)
    upper_behind = passed(upper, 1)
    lower_ahead = passed(lower, -1)
    lower_behind, upper_ahead, meanwhile = lax.optimization_barrier(
        (lower_behind, upper_ahead, meanwhile)
    )
    lower_opposite = passed(lower_behind, 1)
    upper_opposite = passed(upper_ahead, -1)
    return meanwhile, [
        (1, [lower_behind, upper_behind]),
        (3, [lower_ahead, upper_ahead]),
        (2, [lower_opposite, upper_opposite]),
    ]


def body(activations, w_qk, w_value, w_out, bucket_order, span_sends):
    seq_count = lax.axis_size("seq")
    head_count = lax.axis_size("head")
    my_seq = lax.axis_index("seq")
    my_head = lax.axis_index("head")
    me = my_seq.reshape(1).astype(jnp.int32)
    pairs = bucket_order.shape[1] // PAIR
    columns = w_out.shape[1] // head_count

    def send(pieces):
        return lax.all_to_all(pieces, "seq", split_axis=0, concat_axis=0, tiled=True)

    own, arrived = [], []
    for pair in range(pairs):
        rows, sent = project_and_sort(
            me, span_sends, activations, w_qk, w_value, bucket_order, pair
        )
        own.append(rows)
        arrived.append(send(sent.reshape(seq_count, 1, SENT, QUARTER, HEAD_DIM)))

    blocks = []
    for shift in range(head_count):
        at = lax.rem(my_head + shift, head_count) * columns
        block = lax.dynamic_slice_in_dim(w_out, at, columns, axis=1)
        blocks.append(passed(block, shift) if shift else block)
    weights = jnp.stack(blocks)

    of_round = span_sends[my_seq // (2 * PAIR * QUARTERS)]
    of_round = of_round.reshape((pairs, PAIR) + of_round.shape[1:])
    table = left_table(of_round[:, my_seq // (2 * QUARTERS) % PAIR])
    left = []
    for pair in range(pairs):
        pieces = permute(table, arrived[pair], pair)
        pieces, arrived[-1], weights = lax.optimization_barrier((pieces, arrived[-1], weights))
        left.append(send(pieces))

    def attended(pair, parts):
        return attend(me, span_sends, own[pair], left[pair], bucket_order, pair, parts)

    (mine,) = attended(0, 1)
    terms = from_all_groups(mine)
    left[1], rows = lax.optimization_barrier((left[1], [rows for _, rows in terms[:1]]))
    terms[:1] = [(term[0], row) for term, row in zip(terms, rows)]
    halves = attended(1, 2)
    terms = [(0, *term) for term in terms] + [(1, 0, halves)]
    started = project_out(weights, None, terms)
    started, terms = round_the_ring(*halves, started)
    return project_out(weights, started, [(1, *term) for term in terms])


def solution(mesh):
    in_specs = (
        P("seq", None),
        P(None, "head"),
        P(None, "head"),
        P("head", None),
        P(None, "head", "seq"),
        P(None, "head", None, None),
    )
    out_specs = P("seq", "head")
    return jax.shard_map(body, mesh=mesh, in_specs=in_specs, out_specs=out_specs, check_vma=False)
```

```python
import functools
import math

import jax
import jax.numpy as jnp
from jax import lax
from jax.experimental import pallas as pl
from jax.experimental.pallas import tpu as pltpu
from jax.sharding import PartitionSpec as P

HEAD_DIM = 128
SPAN = 64
EPS = 1e-06
SELF_SCORE = -100000.0
QUARTER = 16
QUARTERS = SPAN // QUARTER
PAIR = 2
SENT = 15
VMEM_LIMIT = 64 * 1024 * 1024
OUTPUT_LIMIT = 24 * 1024 * 1024


def params(limit=VMEM_LIMIT):
    return pltpu.CompilerParams(vmem_limit_bytes=limit)


def spare_span(sends_ref, r, head, me):
    counts = sends_ref[r, head, pl.ds(me, 1), :].astype(jnp.float32)
    at = lax.broadcasted_iota(jnp.int32, counts.shape, 1).astype(jnp.float32)
    first = jnp.min(jnp.where(counts > 1.5, at, float(counts.shape[1])))
    before = jnp.sum(jnp.where(at < first, counts, 0.0))
    return jnp.clip(before.astype(jnp.int32), 0, SENT - 1)


def sort_kernel(
    first, me_ref, sends_ref, act_ref, wq_ref, wv_ref, order_ref, out_ref, sent_ref, kv_ref, onehot_ref
):
    tokens = act_ref.shape[0]
    spans = tokens // SPAN
    rounds = out_ref.shape[0]
    head = first + pl.program_id(0)
    lanes = 128
    token_at = lax.broadcasted_iota(jnp.int32, (lanes, tokens), 1).astype(jnp.float32)
    for r in range(rounds):
        row = order_ref[r, pl.ds(head, 1), :].astype(jnp.float32)
        parts = [row[:, j : j + lanes] for j in range(0, tokens, lanes)]
        wanted = jnp.concatenate(parts, axis=0).T
        for j in range(tokens // lanes):
            onehot = jnp.where(wanted[:, j : j + 1] == token_at, 1.0, 0.0)
            onehot_ref[r, j * lanes : (j + 1) * lanes, :] = onehot.astype(jnp.bfloat16)
    weights = jnp.concatenate([wq_ref[...], wv_ref[...]], axis=1)
    kv_ref[...] = jnp.dot(
        act_ref[...], weights, preferred_element_type=jnp.float32
    ).astype(jnp.bfloat16)

    def one_round(r, carry):
        rows = jnp.dot(onehot_ref[r], kv_ref[...], preferred_element_type=jnp.float32)
        rows = rows.astype(jnp.bfloat16)
        for at in range(2):
            half = rows[:, at * HEAD_DIM : (at + 1) * HEAD_DIM]
            half = half.reshape(spans, QUARTERS, QUARTER, HEAD_DIM)
            for quarter in range(QUARTERS):
                out_ref[r, 0, at, quarter, 0] = half[:, quarter]
        spare = spare_span(sends_ref, r, head, me_ref[0])
        for at in range(2):
            tiles = [
                out_ref[r, 0, at, :, 0, j + (j >= spare).astype(jnp.int32)] for j in range(SENT)
            ]
            for j, tile in enumerate(tiles):
                sent_ref[r, 0, at, :, 0, j] = tile
        return carry

    lax.fori_loop(0, rounds, one_round, 0)


def project_and_sort(me, sends, activations, w_qk, w_value, order):
    tokens, width = activations.shape
    rounds, heads = order.shape[:2]
    first = 0
    block = (rounds, 1, 2, QUARTERS, 1, tokens // SPAN, QUARTER, HEAD_DIM)
    shape = (rounds, PAIR, 2, QUARTERS, heads // PAIR) + block[5:]
    return pl.pallas_call(
        functools.partial(sort_kernel, first),
        grid=(heads,),
        in_specs=[
            pl.BlockSpec(memory_space=pltpu.SMEM),
            pl.BlockSpec(sends.shape, lambda h: (0, 0, 0, 0)),
            pl.BlockSpec((tokens, width), lambda h: (0, 0)),
            pl.BlockSpec((width, HEAD_DIM), lambda h: (0, first + h)),
            pl.BlockSpec((width, HEAD_DIM), lambda h: (0, first + h)),
            pl.BlockSpec(order.shape, lambda h: (0, 0, 0)),
        ],
        out_specs=[
            pl.BlockSpec(block, lambda h: (0, h % PAIR, 0, 0, h // PAIR, 0, 0, 0)),
            pl.BlockSpec(
                block[:5] + (SENT,) + block[6:],
                lambda h: (0, h % PAIR, 0, 0, h // PAIR, 0, 0, 0),
            ),
        ],
        out_shape=[
            jax.ShapeDtypeStruct(shape, jnp.bfloat16),
            jax.ShapeDtypeStruct(shape[:5] + (SENT,) + shape[6:], jnp.bfloat16),
        ],
        scratch_shapes=[
            pltpu.VMEM((tokens, 2 * HEAD_DIM), jnp.bfloat16),
            pltpu.VMEM((rounds, tokens, tokens), jnp.bfloat16),
        ],
        compiler_params=params(),
        cost_estimate=pl.CostEstimate(
            flops=heads * tokens * 4 * HEAD_DIM * (width + rounds * tokens),
            bytes_accessed=2 * tokens * width + heads * 4 * HEAD_DIM * (width + 2 * tokens),
            transcendentals=0,
        ),
    )(me, sends, activations, w_qk, w_value, order)


def left_table(counts):
    blocks, ranges = counts.shape[1:]
    spans = SENT + 1
    at = jnp.arange(ranges, dtype=jnp.int32)
    block_at = jnp.arange(blocks, dtype=jnp.int32)
    upto = at[:, None] <= at[None, :]
    inclusive = jnp.sum(jnp.where(upto[None, None], counts[:, :, :, None], 0), axis=2)
    exclusive = inclusive - counts
    spare = jnp.min(jnp.where(counts > 1, exclusive, SENT - 1), axis=2)[:, :, None]
    ends = inclusive - 1
    ends = block_at[None, :, None] * spans + ends - (ends > spare).astype(jnp.int32)
    tails = jnp.where(counts > 0, ends, -1)
    earlier = block_at[:, None] < block_at[None, :]
    before = jnp.max(
        jnp.where(earlier[None, :, :, None], tails[:, :, None, :], -1), axis=1
    )
    last = jnp.max(tails, axis=1)
    wrapped = jnp.roll(last, 1, axis=-1)
    before = jnp.where(before < 0, wrapped[:, None, :], before)
    k_at = jnp.arange(SENT, dtype=jnp.int32)[None, None, :]
    k_at = k_at + (k_at > spare).astype(jnp.int32)
    here = k_at - 1
    here = block_at[None, :, None] * spans + here - (here > spare).astype(jnp.int32)
    k_at, here = k_at[..., None], here[..., None]
    first = exclusive[:, :, None, :]
    mine = (first <= k_at) & (k_at < inclusive[:, :, None, :])
    left = jnp.where(k_at > first, here, before[:, :, None, :])
    left = jnp.sum(jnp.where(mine, left, 0), axis=-1)
    return jnp.clip(left, 0, blocks * spans - 2).reshape(counts.shape[0], blocks * SENT)


def permute_kernel(pair, table_ref, in_ref, out_ref):
    steps, sent = out_ref.shape[:2]
    start = pl.program_id(0) * steps

    def one_block(t, carry):
        tiles = []
        for k in range(sent):
            place = table_ref[pair, (start + t) * sent + k]
            tiles.append(in_ref[place >> 4, 0, place & 15])
        for k, tile in enumerate(tiles):
            out_ref[t, k] = tile
        return carry

    lax.fori_loop(0, steps, one_block, 0, unroll=4)


def permute(table, pieces, pair):
    blocks, _, sent, rows, columns = pieces.shape
    steps = 2
    size = blocks * sent * rows * columns
    return pl.pallas_call(
        functools.partial(permute_kernel, pair),
        grid=(steps,),
        in_specs=[
            pl.BlockSpec(memory_space=pltpu.SMEM),
            pl.BlockSpec((blocks, 1, sent, rows, columns), lambda i: (0, pair, 0, 0, 0)),
        ],
        out_specs=pl.BlockSpec((blocks // steps, sent, rows, columns), lambda i: (i, 0, 0, 0)),
        out_shape=jax.ShapeDtypeStruct((blocks, sent, rows, columns), jnp.bfloat16),
        compiler_params=params(),
        cost_estimate=pl.CostEstimate(flops=size, bytes_accessed=4 * size, transcendentals=0),
    )(table, pieces)


def as_spans(quarters):
    spans = quarters.shape[1]
    return jnp.swapaxes(quarters, 0, 1).reshape(spans, SPAN, HEAD_DIM)


def batched(left, right, left_dim, right_dim):
    return lax.dot_general(
        left,
        right,
        (((left_dim,), (right_dim,)), ((0,), (0,))),
        preferred_element_type=jnp.float32,
    )


def attend_kernel(
    first, me_ref, sends_ref, own_ref, left_ref, order_ref, *refs
):
    *out_refs, mixed_ref, all_ref = refs
    rounds, _, tokens = order_ref.shape
    head = first + pl.program_id(0)
    spans = tokens // SPAN
    for r in range(rounds):
        spare = spare_span(sends_ref, r, head, me_ref[0])
        for at in range(2):
            tiles = [left_ref[r, 0, at, :, j] for j in range(SENT)]
            tiles.append(own_ref[r, 0, at, :, 0, spare])
            for j, tile in enumerate(tiles[:-1]):
                all_ref[r, at, :, j + (j > spare).astype(jnp.int32)] = tile
            all_ref[r, at, :, spare + 1] = tiles[-1]
        queries = as_spans(own_ref[r, 0, 0, :, 0])
        keys = jnp.concatenate([as_spans(all_ref[r, 0]), queries], axis=1)
        values = jnp.concatenate([as_spans(all_ref[r, 1]), as_spans(own_ref[r, 0, 1, :, 0])], axis=1)
        scores = batched(queries, keys, 2, 2)
        wide = keys.astype(jnp.float32)
        squares = wide * wide
        sums = jnp.sum(squares, axis=2)[:, None, :]
        scaling = lax.rsqrt(sums + EPS) * (1.0 / math.sqrt(HEAD_DIM))
        scores = scores * scaling
        query_at = lax.broadcasted_iota(jnp.int32, scores.shape, 1)
        key_at = lax.broadcasted_iota(jnp.int32, scores.shape, 2)
        scores = jnp.where(key_at == query_at + SPAN, SELF_SCORE, scores)
        summit = jnp.max(scores, axis=-1, keepdims=True)
        raised = jnp.exp(scores - summit)
        totals = jnp.sum(raised, axis=-1, keepdims=True)
        weights = (raised * (1.0 / totals)).astype(jnp.bfloat16)
        mixed = batched(weights, values, 2, 1).astype(jnp.bfloat16)
        log_total = summit + jnp.log(totals)
        high = log_total.astype(jnp.bfloat16).astype(jnp.float32)
        middle = (log_total - high).astype(jnp.bfloat16).astype(jnp.float32)
        low = log_total - high - middle
        lane = lax.broadcasted_iota(jnp.int32, scores.shape, 2)
        terms = jnp.where(lane == 0, high, jnp.where(lane == 1, middle, low))
        terms = jnp.where(lane < 3, terms, 0.0).astype(jnp.bfloat16)
        mixed_ref[r, :, :HEAD_DIM] = mixed.reshape(tokens, HEAD_DIM)
        mixed_ref[r, :, HEAD_DIM:] = terms.reshape(tokens, HEAD_DIM)
    step = 256
    token_at = lax.broadcasted_iota(jnp.int32, (step, tokens), 0)
    for lower in range(0, tokens, step):
        rows, totals = [], []
        for r in range(rounds):
            onehot = order_ref[r, pl.ds(head, 1), :] == token_at + lower
            onehot = jnp.where(onehot, 1.0, 0.0).astype(jnp.bfloat16)
            found = jnp.dot(onehot, mixed_ref[r], preferred_element_type=jnp.float32)
            rows.append(found[:, :HEAD_DIM])
            totals.append(
                found[:, HEAD_DIM : HEAD_DIM + 1]
                + found[:, HEAD_DIM + 1 : HEAD_DIM + 2]
                + found[:, HEAD_DIM + 2 : HEAD_DIM + 3]
            )
        peak = functools.reduce(jnp.maximum, totals)
        shares = [jnp.exp(total - peak) for total in totals]
        inverse = 1.0 / functools.reduce(jnp.add, shares)
        blended = functools.reduce(
            jnp.add, [(share * inverse) * row for share, row in zip(shares, rows)]
        )
        share = tokens // len(out_refs)
        out_ref, at = out_refs[lower // share], lower % share
        out_ref[at : at + step, :] = blended.astype(jnp.bfloat16)


def attend(me, sends, own, left, order, pair, parts):
    rounds, _, tokens = order.shape
    block = (rounds, 1, 2, QUARTERS, 1) + own.shape[5:]
    share = tokens // parts
    part = jax.ShapeDtypeStruct((share, PAIR * HEAD_DIM), jnp.bfloat16)
    return pl.pallas_call(
        functools.partial(attend_kernel, PAIR * pair),
        grid=(PAIR,),
        in_specs=[
            pl.BlockSpec(memory_space=pltpu.SMEM),
            pl.BlockSpec(sends.shape, lambda h: (0, 0, 0, 0)),
            pl.BlockSpec(block, lambda h: (0, h, 0, 0, pair, 0, 0, 0)),
            pl.BlockSpec(block[:4] + left.shape[1:], lambda h: (0, h, 0, 0, 0, 0, 0)),
            pl.BlockSpec(order.shape, lambda h: (0, 0, 0)),
        ],
        out_specs=[pl.BlockSpec((share, HEAD_DIM), lambda h: (0, h))] * parts,
        out_shape=[part] * parts,
        scratch_shapes=[
            pltpu.VMEM((rounds, tokens, 2 * HEAD_DIM), jnp.bfloat16),
            pltpu.VMEM((rounds, 2, QUARTERS) + own.shape[5:], jnp.bfloat16),
        ],
        compiler_params=params(),
        cost_estimate=pl.CostEstimate(
            flops=PAIR * rounds * tokens * 4 * HEAD_DIM * (tokens + 2 * SPAN),
            bytes_accessed=PAIR * rounds * tokens * 8 * HEAD_DIM,
            transcendentals=PAIR * rounds * tokens * 2 * SPAN,
        ),
    )(me, sends, own, left.reshape(own.shape[:4] + left.shape[1:]), order)


def output_kernel(started, parts, *refs):
    out_ref = refs[-1]
    lower_half = pl.program_id(0) < pl.num_programs(0) // 2
    total = refs[0][...] if started else jnp.zeros(out_ref.shape, jnp.float32)
    at = int(started)
    for count in parts:
        rows = refs[at + 1][...]
        if count == 2:
            rows = jnp.where(lower_half, rows, refs[at + 2][...])
        total += jnp.dot(rows, refs[at][0], preferred_element_type=jnp.float32)
        at += 1 + count
    out_ref[...] = total.astype(out_ref.dtype)


def project_out(weights, started, terms):
    columns = weights.shape[2]
    tokens = sum(rows.shape[0] for rows in terms[0][2])
    depth = terms[0][2][0].shape[1]
    steps = 2
    step = tokens // steps
    whole = lambda i: (i, 0)
    lower = lambda i: (jnp.minimum(i, steps // 2 - 1), 0)
    upper = lambda i: (jnp.maximum(i - steps // 2, 0), 0)
    in_specs, operands = [], []
    if started is not None:
        in_specs.append(pl.BlockSpec((step, columns), whole))
        operands.append(started)
    for pair, behind, rows in terms:
        in_specs.append(pl.BlockSpec((1, depth, columns), lambda i, at=(behind, pair, 0): at))
        for where in [whole] if len(rows) == 1 else [lower, upper]:
            in_specs.append(pl.BlockSpec((step, depth), where))
        operands += [weights, *rows]
    kind = jnp.float32 if started is None else jnp.bfloat16
    return pl.pallas_call(
        functools.partial(output_kernel, started is not None, [len(t[2]) for t in terms]),
        grid=(steps,),
        in_specs=in_specs,
        out_specs=pl.BlockSpec((step, columns), whole),
        out_shape=jax.ShapeDtypeStruct((tokens, columns), kind),
        compiler_params=params(OUTPUT_LIMIT),
        cost_estimate=pl.CostEstimate(
            flops=2 * len(terms) * tokens * depth * columns,
            bytes_accessed=2 * len(terms) * depth * (tokens + columns) + 6 * tokens * columns,
            transcendentals=0,
        ),
    )(*operands)


def passed(array, by):
    count = lax.axis_size("head")
    return lax.ppermute(array, "head", [(i, (i + by) % count) for i in range(count)])


def from_all_groups(mine):
    return [(0, [mine]), (1, [passed(mine, 1)]), (3, [passed(mine, -1)]), (2, [passed(mine, 2)])]


def round_the_ring(lower, upper, meanwhile):
    lower_behind = passed(lower, 1)
    upper_ahead = passed(upper, -1)
    upper_behind = passed(upper, 1)
    lower_ahead = passed(lower, -1)
    lower_behind, upper_ahead, meanwhile = lax.optimization_barrier(
        (lower_behind, upper_ahead, meanwhile)
    )
    lower_opposite = passed(lower_behind, 1)
    upper_opposite = passed(upper_ahead, -1)
    return meanwhile, [
        (1, [lower_behind, upper_behind]),
        (3, [lower_ahead, upper_ahead]),
        (2, [lower_opposite, upper_opposite]),
    ]


def body(activations, w_qk, w_value, w_out, bucket_order, span_sends):
    seq_count = lax.axis_size("seq")
    head_count = lax.axis_size("head")
    my_seq = lax.axis_index("seq")
    my_head = lax.axis_index("head")
    me = my_seq.reshape(1).astype(jnp.int32)
    pairs = bucket_order.shape[1] // PAIR
    columns = w_out.shape[1] // head_count

    def send(pieces):
        return lax.all_to_all(pieces, "seq", split_axis=0, concat_axis=0, tiled=True)

    own, sent = project_and_sort(me, span_sends, activations, w_qk, w_value, bucket_order)
    arrived = send(sent.reshape(seq_count, pairs, SENT, QUARTER, HEAD_DIM))

    blocks = []
    for shift in range(head_count):
        at = lax.rem(my_head + shift, head_count) * columns
        block = lax.dynamic_slice_in_dim(w_out, at, columns, axis=1)
        blocks.append(passed(block, shift) if shift else block)
    weights = jnp.stack(blocks)

    of_round = span_sends[my_seq // (2 * PAIR * QUARTERS)]
    of_round = of_round.reshape((pairs, PAIR) + of_round.shape[1:])
    table = left_table(of_round[:, my_seq // (2 * QUARTERS) % PAIR])
    left = []
    for pair in range(pairs):
        pieces = permute(table, arrived, pair)
        pieces, arrived, weights = lax.optimization_barrier((pieces, arrived, weights))
        left.append(send(pieces))

    def attended(pair, parts):
        return attend(me, span_sends, own, left[pair], bucket_order, pair, parts)

    (mine,) = attended(0, 1)
    terms = from_all_groups(mine)
    left[1], rows = lax.optimization_barrier((left[1], [rows for _, rows in terms[:1]]))
    terms[:1] = [(term[0], row) for term, row in zip(terms, rows)]
    halves = attended(1, 2)
    terms = [(0, *term) for term in terms] + [(1, 0, halves)]
    started = project_out(weights, None, terms)
    started, terms = round_the_ring(*halves, started)
    return project_out(weights, started, [(1, *term) for term in terms])


def solution(mesh):
    in_specs = (
        P("seq", None),
        P(None, "head"),
        P(None, "head"),
        P("head", None),
        P(None, "head", "seq"),
        P(None, "head", None, None),
    )
    out_specs = P("seq", "head")
    return jax.shard_map(body, mesh=mesh, in_specs=in_specs, out_specs=out_specs, check_vma=False)
```
